32 devices in a mesh: gy: 8 (over z, core), gz: 4 (over y, x).
Axes of the slice: x: 2, y: 2, z: 4, core: 2. Of those that a mesh axis runs over, the one named last changes fastest.
Arguments:
- adjoint: float32 [5, 32, 1024, 256], P(None, 'gz', 'gy'), may hold values from -6 to 6
- speed: float32 [32, 1024, 256], P('gz', 'gy'), may hold values from 0.5 to 2
- x_derivative: float32 [256, 256], replicated, may hold values from -0.375 to 0.375
- y_operators: float32 [2, 1024, 1024], replicated, may hold values from -0.1875 to 0.1875
- coupling: float32 [3, 5, 5], replicated, may hold values from -2.5 to 2.5
Outputs:
- advanced: float32 [5, 32, 1024, 256], P(None, 'gz', 'gy')
The draws below stay inside these ranges and needn't reach their ends.
All inputs are finite; a program needn't handle non-finite values.
Results may differ from the reference program's by a relative error of at most 0.0001.
Values sent between devices are 32-bit elements; how exact they have to be, the bound alone decides.
A program may use at most 128 MiB of HBM per device.

```python
import math
import jax
import jax.numpy as jnp
from jax import lax

FIELDS = 5
NX = 256
NY = 1024
NZ = 32


def block_levels(own_key, dims, shards, low, high):
    def one(position, parts):
        heights = jax.random.uniform(jax.random.fold_in(jax.random.fold_in(own_key, 6), position), (parts,), jnp.float32, low / len(shards), high / len(shards))
        return jnp.repeat(jnp.exp(heights), dims[position] // parts).reshape((-1,) + (1,) * (len(dims) - position - 1))

    level = one(*shards[0])
    for cut in shards[1:]:
        level = level * one(*cut)
    return level


def bell_draw(stream_key, extent, deviation, limit, cuts=(), held_as=jnp.bfloat16):
    gain = block_levels(stream_key, extent, cuts, -0.22, 0.18) if cuts else 1.0
    array = jax.random.normal(stream_key, extent, jnp.float32) * deviation * gain
    return jnp.minimum(jnp.maximum(array, -limit), limit).astype(held_as)


def setup_inputs(seed: int = 0) -> dict:
    key_list = jax.random.split(jax.random.key(seed), 6)
    return {
        "adjoint": bell_draw(key_list[0], (FIELDS, NZ, NY, NX), 1.0, 6.0, ((1, 4), (2, 8)), jnp.float32),
        "speed": jnp.clip(jnp.exp(math.log(2.0) - 1.3862944 * jax.random.uniform(key_list[1], (NZ, NY, NX), jnp.float32) ** block_levels(key_list[1], (NZ, NY, NX), ((0, 4), (1, 8)), -0.2, 0.2)), 0.5, 2.0),
        "x_derivative": bell_draw(key_list[2], (NX, NX), NX ** -0.5, 0.375, (), jnp.float32),
        "y_operators": bell_draw(key_list[3], (2, NY, NY), NY ** -0.5, 0.1875, (), jnp.float32),
        "coupling": bell_draw(key_list[4], (3, FIELDS, FIELDS), FIELDS ** -0.5, 2.5, (), jnp.float32),
    }


stencil = (0.8, -0.2, 4.0 / 105.0, -1.0 / 280.0)
viscous = 0.5
stepping = 0.5


def reference(adjoint, speed, x_derivative, y_operators, coupling):
    highest = lax.Precision.HIGHEST

    def one_field(carry, index):
        advect, curves = carry
        field = lax.dynamic_index_in_dim(adjoint, index, 0, keepdims=False)
        grad_x = jnp.einsum('zyk,xk->zyx', field, x_derivative, precision=highest)
        grad_y = jnp.einsum('yk,zkx->zyx', y_operators[0], field, precision=highest)
        curve_y = jnp.einsum('yk,zkx->zyx', y_operators[1], field, precision=highest)
        grad_z = jnp.zeros_like(field)
        for step, weight in enumerate(stencil):
            shift = step + 1
            grad_z = grad_z + weight * (jnp.roll(field, -shift, axis=0) - jnp.roll(field, shift, axis=0))
        column = lax.dynamic_index_in_dim(coupling, index, 1, keepdims=False)
        advect = (advect + column[0][:, None, None, None] * grad_x[None]
                  + column[1][:, None, None, None] * grad_y[None]
                  + column[2][:, None, None, None] * grad_z[None])
        curves = lax.dynamic_update_index_in_dim(curves, curve_y, index, 0)
        return (advect, curves), None

    start = (jnp.zeros(adjoint.shape, jnp.float32), jnp.zeros(adjoint.shape, jnp.float32))
    (advect, curves), unused = lax.scan(one_field, start, jnp.arange(adjoint.shape[0], dtype=jnp.int32))
    rhs = speed[None] * advect + viscous * curves
    return adjoint + stepping * rhs
```

```python
import functools

import jax
import jax.numpy as jnp
from jax import lax
from jax.experimental import pallas as pl
from jax.experimental.pallas import tpu as pltpu
from jax.sharding import PartitionSpec as P

stencil = (0.8, -0.2, 4.0 / 105.0, -1.0 / 280.0)
viscous = 0.5
stepping = 0.5
MESH = pl.DeviceIdType.MESH
LANES = 128


def split(values):
    high = values.astype(jnp.bfloat16)
    low = (values - high.astype(jnp.float32)).astype(jnp.bfloat16)
    return high, low


def y_kernel(
    n, nz, adjoint, speed, y_ops, coupling, terms, halos,
    gath, speeds, op_stage, lhs, rhs_high, rhs_low, outgo,
    gather_send, gather_recv, forward_send, forward_recv, back_send, back_recv,
    speed_send, speed_recv, halo_send, halo_recv, local_sem, op_sem,
):
    fields, depth, rows, width = adjoint.shape
    half_n = n // 2
    workers = n // 4
    planes = depth // workers
    cuts = width // LANES
    chunks = planes * cuts
    me = lax.axis_index("gy")
    mz = lax.axis_index("gz")
    half = me // half_n
    mine = me - half * half_n
    base = half * half_n
    first_worker = base + (1 - half) * workers
    rank = me - first_worker
    is_worker = jnp.logical_and(rank >= 0, rank < workers)
    partner = me + (1 - 2 * half) * workers
    above, below = lax.rem(mz + 1, nz), lax.rem(mz + nz - 1, nz)
    extent = y_ops.shape[1]
    half_rows = extent // 2

    barrier = pltpu.get_barrier_semaphore()
    for side in (above, below):
        pl.semaphore_signal(barrier, inc=1, device_id=(me, side), device_id_type=MESH)

    @pl.when(is_worker)
    def _():
        def greet(i, carry):
            @pl.when(base + i != me)
            def _():
                pl.semaphore_signal(barrier, inc=1, device_id=(base + i, mz), device_id_type=MESH)
            return carry
        lax.fori_loop(0, half_n, greet, 0)
        pl.semaphore_signal(barrier, inc=1, device_id=(partner, mz), device_id_type=MESH)
        pl.semaphore_wait(barrier, half_n + 2)

    @pl.when(jnp.logical_not(is_worker))
    def _():
        def greet(i, carry):
            pl.semaphore_signal(barrier, inc=1, device_id=(first_worker + i, mz), device_id_type=MESH)
            return carry
        lax.fori_loop(0, workers, greet, 0)
        pl.semaphore_wait(barrier, workers + 2)

    def piece(ref, worker, chunk):
        plane = worker * planes + chunk // cuts
        lane = pl.multiple_of(lax.rem(chunk, cuts) * LANES, LANES)
        return ref.at[:, plane, :, pl.ds(lane, LANES)]

    def gather(worker, chunk):
        return pltpu.make_async_remote_copy(
            src_ref=piece(adjoint, worker, chunk), dst_ref=gath.at[chunk, me],
            send_sem=gather_send.at[worker, chunk], recv_sem=gather_recv.at[mine, chunk],
            device_id=(first_worker + worker, mz), device_id_type=MESH)

    def gathered(i, chunk):
        return pltpu.make_async_remote_copy(
            src_ref=gath.at[chunk, base + i], dst_ref=gath.at[chunk, base + i],
            send_sem=gather_send.at[0, chunk], recv_sem=gather_recv.at[i, chunk],
            device_id=(partner, mz), device_id_type=MESH)

    def forward(i, chunk):
        return pltpu.make_async_remote_copy(
            src_ref=gath.at[chunk, base + i], dst_ref=gath.at[chunk, base + i],
            send_sem=forward_send.at[i, chunk], recv_sem=forward_recv.at[i, chunk],
            device_id=(partner, mz), device_id_type=MESH)

    def forwarded(i, chunk):
        other = (1 - half) * half_n + i
        return pltpu.make_async_remote_copy(
            src_ref=gath.at[chunk, other], dst_ref=gath.at[chunk, other],
            send_sem=forward_send.at[i, chunk], recv_sem=forward_recv.at[i, chunk],
            device_id=(partner, mz), device_id_type=MESH)

    def own(chunk):
        return pltpu.make_async_copy(piece(adjoint, rank, chunk), gath.at[chunk, me], local_sem.at[chunk])

    def speed_copy(worker):
        return pltpu.make_async_remote_copy(
            src_ref=speed.at[pl.ds(worker * planes, planes)], dst_ref=speeds.at[mine],
            send_sem=speed_send.at[worker], recv_sem=speed_recv.at[mine],
            device_id=(first_worker + worker, mz), device_id_type=MESH)

    def speed_arrival(i):
        return pltpu.make_async_remote_copy(
            src_ref=speed.at[pl.ds(0, planes)], dst_ref=speeds.at[i],
            send_sem=speed_send.at[0], recv_sem=speed_recv.at[i],
            device_id=(partner, mz), device_id_type=MESH)

    def back(i, chunk, slot):
        return pltpu.make_async_remote_copy(
            src_ref=outgo.at[slot, i], dst_ref=piece(terms, rank, chunk),
            send_sem=back_send.at[i, slot], recv_sem=back_recv.at[rank, chunk],
            device_id=(base + i, mz), device_id_type=MESH)

    def back_own(chunk, slot):
        return pltpu.make_async_copy(
            outgo.at[slot, mine], piece(terms, rank, chunk), back_send.at[mine, slot])

    def back_arrival(worker, chunk):
        return pltpu.make_async_remote_copy(
            src_ref=outgo.at[0, 0], dst_ref=piece(terms, worker, chunk),
            send_sem=back_send.at[0, 0], recv_sem=back_recv.at[worker, chunk],
            device_id=(first_worker + worker, mz), device_id_type=MESH)

    reach = halos.shape[2]
    halo_up = pltpu.make_async_remote_copy(
        src_ref=adjoint.at[:, pl.ds(depth - reach, reach)], dst_ref=halos.at[0],
        send_sem=halo_send.at[0], recv_sem=halo_recv.at[0],
        device_id=(me, above), device_id_type=MESH)
    halo_down = pltpu.make_async_remote_copy(
        src_ref=adjoint.at[:, pl.ds(0, reach)], dst_ref=halos.at[1],
        send_sem=halo_send.at[1], recv_sem=halo_recv.at[1],
        device_id=(me, below), device_id_type=MESH)

    def each(count, body):
        def step(i, carry):
            body(i)
            return carry
        lax.fori_loop(0, count, step, 0)

    @pl.when(jnp.logical_not(is_worker))
    def _():
        def send(chunk):
            @pl.when(chunk >= 2)
            def _():
                each(workers, lambda w: gather(w, chunk - 2).wait_send())
            each(workers, lambda w: gather(w, chunk).start())

            @pl.when(chunk == 0)
            def _():
                each(workers, lambda w: speed_copy(w).start())
                halo_up.start()
                halo_down.start()
        each(chunks, send)
        for last in (chunks - 2, chunks - 1):
            each(workers, lambda w: gather(w, last).wait_send())
        each(workers, lambda w: speed_copy(w).wait_send())
        each(chunks, lambda c: each(workers, lambda w: back_arrival(w, c).wait_recv()))

    @pl.when(is_worker)
    def _():
        def to_mates(chunk):
            def one(w):
                @pl.when(w != rank)
                def _():
                    gather(w, chunk).start()
            each(workers, one)
            own(chunk).start()
        each(chunks, to_mates)

        def mates(fn):
            def one(w):
                @pl.when(w != rank)
                def _():
                    fn(w)
            each(workers, one)

        def others(fn):
            def one(i):
                @pl.when(i != mine)
                def _():
                    fn(i)
            each(half_n, one)

        mates(lambda w: speed_copy(w).start())
        own_speed = pltpu.make_async_copy(
            speed.at[pl.ds(rank * planes, planes)], speeds.at[mine], op_sem.at[1])
        own_speed.start()
        op_row = pl.multiple_of(half * half_rows, half_rows)
        op_copy = pltpu.make_async_copy(
            y_ops.at[:, pl.ds(op_row, half_rows)], op_stage, op_sem.at[0])
        op_copy.start()

        def send_forward(chunk):
            own(chunk).wait()
            forward(mine, chunk).start()

            def step(k):
                i = lax.rem(k + (1 - half) * workers, half_n)

                @pl.when(i != mine)
                def _():
                    gathered(i, chunk).wait_recv()
                    forward(i, chunk).start()
            each(half_n, step)

        send_forward(0)
        halo_up.start()
        halo_down.start()
        op_copy.wait()

        def prepare(i):
            top = pl.multiple_of(i * rows, rows)
            for op in range(2):
                high, low = split(op_stage[op, pl.ds(top, rows), :])
                lhs[i, op * rows:(op + 1) * rows, :] = high
                lhs[i, (2 + op) * rows:(3 + op) * rows, :] = low
        each(half_n, prepare)
        own_speed.wait()
        others(lambda i: speed_arrival(i).wait_recv())

        def work(chunk):
            @pl.when(chunk + 1 < chunks)
            def _():
                @pl.when(chunk >= 1)
                def _():
                    each(half_n, lambda i: forward(i, chunk - 1).wait_send())
                send_forward(chunk + 1)

            each(half_n, lambda i: forwarded(i, chunk).wait_recv())

            def convert(b):
                top = pl.multiple_of(b * rows, rows)
                for f in range(fields):
                    high, low = split(gath[chunk, b, f])
                    rhs_high[pl.ds(top, rows), f * LANES:(f + 1) * LANES] = high
                    rhs_low[pl.ds(top, rows), f * LANES:(f + 1) * LANES] = low
            each(n, convert)
            slot = lax.rem(chunk, 2)
            plane = chunk // cuts
            lane = pl.multiple_of(lax.rem(chunk, cuts) * LANES, LANES)

            @pl.when(chunk >= 2)
            def _():
                others(lambda i: back(i, chunk - 2, slot).wait_send())
                back_own(chunk - 2, slot).wait()

            def produce(k):
                i = k + half * (half_n - 1 - 2 * k)
                full = jnp.dot(lhs[i], rhs_high[...], preferred_element_type=jnp.float32)
                rest = jnp.dot(lhs[i, :2 * rows], rhs_low[...], preferred_element_type=jnp.float32)
                both = full[:2 * rows] + full[2 * rows:] + rest
                pace = speeds[i, plane, :, pl.ds(lane, LANES)]
                for f in range(fields):
                    total = coupling[1, 0, f] * both[:rows, :LANES]
                    for g in range(1, fields):
                        total = total + coupling[1, g, f] * both[:rows, g * LANES:(g + 1) * LANES]
                    outgo[slot, i, f] = pace * total + viscous * both[rows:, f * LANES:(f + 1) * LANES]

                @pl.when(i != mine)
                def _():
                    back(i, chunk, slot).start()

                @pl.when(i == mine)
                def _():
                    back_own(chunk, slot).start()
            each(half_n, produce)
        each(chunks, work)

        for last in (chunks - 2, chunks - 1):
            each(half_n, lambda i: forward(i, last).wait_send())
            others(lambda i: back(i, last, last % 2).wait_send())
            back_own(last, last % 2).wait()
        each(chunks, lambda c: mates(lambda w: gather(w, c).wait_send()))
        mates(lambda w: speed_copy(w).wait_send())
        each(chunks, lambda c: mates(lambda w: back_arrival(w, c).wait_recv()))

    halo_up.wait()
    halo_down.wait()


def local_kernel(adjoint, halos, speed, x_op, coupling, terms, out, ext, along):
    fields, depth, rows, width = adjoint.shape
    reach = len(stencil)
    ext[:, :reach] = halos[0]
    ext[:, reach:reach + depth] = adjoint[...]
    ext[:, reach + depth:] = halos[1]
    x_high, x_low = split(x_op[...])
    contract = (((1,), (1,)), ((), ()))

    def times(left, right):
        return lax.dot_general(left, right, contract, preferred_element_type=jnp.float32)

    for f in range(fields):
        high, low = split(adjoint[f].reshape(depth * rows, width))
        product = times(high, x_high) + times(high, x_low) + times(low, x_high)
        along[f] = product.reshape(depth, rows, width)

    def plane(p, carry):
        across = []
        for g in range(fields):
            total = None
            for step, weight in enumerate(stencil):
                part = weight * (ext[g, p + reach + step + 1] - ext[g, p + reach - step - 1])
                total = part if total is None else total + part
            across.append(total)
        pace = speed[p]
        for f in range(fields):
            total = coupling[0, 0, f] * along[0, p] + coupling[2, 0, f] * across[0]
            for g in range(1, fields):
                total = total + coupling[0, g, f] * along[g, p] + coupling[2, g, f] * across[g]
            out[f, p] = adjoint[f, p] + stepping * (pace * total + terms[f, p])
        return carry
    lax.fori_loop(0, depth, plane, 0)


def shards(n, nz, adjoint, speed, x_derivative, y_operators, coupling):
    fields, depth, rows, width = adjoint.shape
    half_n, workers = n // 2, n // 4
    planes = depth // workers
    chunks = planes * (width // LANES)
    reach = len(stencil)
    extent = y_operators.shape[1]
    f32, bf16 = jnp.float32, jnp.bfloat16
    dma = pltpu.SemaphoreType.DMA
    hbm = pl.BlockSpec(memory_space=pl.ANY)
    smem = pl.BlockSpec(memory_space=pltpu.SMEM)
    terms, halos = pl.pallas_call(
        functools.partial(y_kernel, n, nz),
        out_shape=(
            jax.ShapeDtypeStruct(adjoint.shape, f32),
            jax.ShapeDtypeStruct((2, fields, reach, rows, width), f32),
        ),
        in_specs=[hbm, hbm, hbm, smem],
        out_specs=(hbm, hbm),
        scratch_shapes=[
            pltpu.VMEM((chunks, n, fields, rows, LANES), f32),
            pltpu.VMEM((half_n, planes, rows, width), f32),
            pltpu.VMEM((2, extent // 2, extent), f32),
            pltpu.VMEM((half_n, 4 * rows, extent), bf16),
            pltpu.VMEM((extent, fields * LANES), bf16),
            pltpu.VMEM((extent, fields * LANES), bf16),
            pltpu.VMEM((2, half_n, fields, rows, LANES), f32),
            dma((workers, chunks)), dma((half_n, chunks)),
            dma((half_n, chunks)), dma((half_n, chunks)),
            dma((half_n, 2)), dma((workers, chunks)),
            dma((workers,)), dma((half_n,)),
            dma((2,)), dma((2,)), dma((chunks,)), dma((2,)),
        ],
        compiler_params=pltpu.CompilerParams(
            collective_id=0, has_side_effects=True, vmem_limit_bytes=56 * 2**20),
        cost_estimate=pl.CostEstimate(
            flops=12 * fields * depth * rows * width * extent,
            bytes_accessed=16 * fields * depth * rows * width, transcendentals=0),
    )(adjoint, speed, y_operators, coupling)

    tile = 16
    block = pl.BlockSpec((fields, depth, tile, width), lambda i: (0, 0, i, 0))
    return pl.pallas_call(
        local_kernel,
        grid=(rows // tile,),
        out_shape=jax.ShapeDtypeStruct(adjoint.shape, f32),
        in_specs=[
            block,
            pl.BlockSpec((2, fields, reach, tile, width), lambda i: (0, 0, 0, i, 0)),
            pl.BlockSpec((depth, tile, width), lambda i: (0, i, 0)),
            pl.BlockSpec((width, width), lambda i: (0, 0)),
            smem,
            block,
        ],
        out_specs=block,
        scratch_shapes=[
            pltpu.VMEM((fields, depth + 2 * reach, tile, width), f32),
            pltpu.VMEM((fields, depth, tile, width), f32),
        ],
        compiler_params=pltpu.CompilerParams(vmem_limit_bytes=40 * 2**20),
        cost_estimate=pl.CostEstimate(
            flops=6 * fields * depth * rows * width * width,
            bytes_accessed=20 * fields * depth * rows * width, transcendentals=0),
    )(adjoint, halos, speed, x_derivative, coupling, terms)


def solution(mesh):
    placed = (P(None, "gz", "gy", None), P("gz", "gy", None), P(), P(), P())
    body = functools.partial(shards, mesh.shape["gy"], mesh.shape["gz"])
    return jax.shard_map(
        body, mesh=mesh, in_specs=placed, out_specs=P(None, "gz", "gy", None), check_vma=False
    )
```

```python
import functools

import jax
import jax.numpy as jnp
from jax import lax
from jax.experimental import pallas as pl
from jax.experimental.pallas import tpu as pltpu
from jax.sharding import PartitionSpec as P

stencil = (0.8, -0.2, 4.0 / 105.0, -1.0 / 280.0)
viscous = 0.5
stepping = 0.5
MESH = pl.DeviceIdType.MESH
LANES = 128
TILE = 16


def split(values):
    high = values.astype(jnp.bfloat16)
    low = (values - high.astype(jnp.float32)).astype(jnp.bfloat16)
    return high, low


def y_kernel(
    n, nz, adjoint, speed, y_ops, x_op, coupling, terms, halos, local,
    gath, speeds, op_stage, lhs, rhs_high, rhs_low, outgo,
    x_mat, ext, along, pace_tile, result,
    gather_send, gather_recv, forward_send, forward_recv, back_send, back_recv,
    speed_send, speed_recv, halo_send, halo_recv, local_sem, op_sem, tile_sem,
):
    fields, depth, rows, width = adjoint.shape
    half_n = n // 2
    workers = n // 4
    planes = depth // workers
    cuts = width // LANES
    chunks = planes * cuts
    me = lax.axis_index("gy")
    mz = lax.axis_index("gz")
    half = me // half_n
    mine = me - half * half_n
    base = half * half_n
    first_worker = base + (1 - half) * workers
    rank = me - first_worker
    is_worker = jnp.logical_and(rank >= 0, rank < workers)
    partner = me + (1 - 2 * half) * workers
    above, below = lax.rem(mz + 1, nz), lax.rem(mz + nz - 1, nz)
    extent = y_ops.shape[1]
    half_rows = extent // 2

    barrier = pltpu.get_barrier_semaphore()
    for side in (above, below):
        pl.semaphore_signal(barrier, inc=1, device_id=(me, side), device_id_type=MESH)

    @pl.when(is_worker)
    def _():
        def greet(i, carry):
            @pl.when(base + i != me)
            def _():
                pl.semaphore_signal(barrier, inc=1, device_id=(base + i, mz), device_id_type=MESH)
            return carry
        lax.fori_loop(0, half_n, greet, 0)
        pl.semaphore_signal(barrier, inc=1, device_id=(partner, mz), device_id_type=MESH)
        pl.semaphore_wait(barrier, half_n + 2)

    @pl.when(jnp.logical_not(is_worker))
    def _():
        def greet(i, carry):
            pl.semaphore_signal(barrier, inc=1, device_id=(first_worker + i, mz), device_id_type=MESH)
            return carry
        lax.fori_loop(0, workers, greet, 0)
        pl.semaphore_wait(barrier, workers + 2)

    def piece(ref, worker, chunk):
        plane = worker * planes + chunk // cuts
        lane = pl.multiple_of(lax.rem(chunk, cuts) * LANES, LANES)
        return ref.at[:, plane, :, pl.ds(lane, LANES)]

    def gather(worker, chunk):
        return pltpu.make_async_remote_copy(
            src_ref=piece(adjoint, worker, chunk), dst_ref=gath.at[chunk, me],
            send_sem=gather_send.at[worker, chunk], recv_sem=gather_recv.at[mine, chunk],
            device_id=(first_worker + worker, mz), device_id_type=MESH)

    def gathered(i, chunk):
        return pltpu.make_async_remote_copy(
            src_ref=gath.at[chunk, base + i], dst_ref=gath.at[chunk, base + i],
            send_sem=gather_send.at[0, chunk], recv_sem=gather_recv.at[i, chunk],
            device_id=(partner, mz), device_id_type=MESH)

    def forward(i, chunk):
        return pltpu.make_async_remote_copy(
            src_ref=gath.at[chunk, base + i], dst_ref=gath.at[chunk, base + i],
            send_sem=forward_send.at[i, chunk], recv_sem=forward_recv.at[i, chunk],
            device_id=(partner, mz), device_id_type=MESH)

    def forwarded(i, chunk):
        other = (1 - half) * half_n + i
        return pltpu.make_async_remote_copy(
            src_ref=gath.at[chunk, other], dst_ref=gath.at[chunk, other],
            send_sem=forward_send.at[i, chunk], recv_sem=forward_recv.at[i, chunk],
            device_id=(partner, mz), device_id_type=MESH)

    def own(chunk):
        return pltpu.make_async_copy(piece(adjoint, rank, chunk), gath.at[chunk, me], local_sem.at[chunk])

    def speed_copy(worker):
        return pltpu.make_async_remote_copy(
            src_ref=speed.at[pl.ds(worker * planes, planes)], dst_ref=speeds.at[mine],
            send_sem=speed_send.at[worker], recv_sem=speed_recv.at[mine],
            device_id=(first_worker + worker, mz), device_id_type=MESH)

    def speed_arrival(i):
        return pltpu.make_async_remote_copy(
            src_ref=speed.at[pl.ds(0, planes)], dst_ref=speeds.at[i],
            send_sem=speed_send.at[0], recv_sem=speed_recv.at[i],
            device_id=(partner, mz), device_id_type=MESH)

    def back(i, chunk, slot):
        return pltpu.make_async_remote_copy(
            src_ref=outgo.at[slot, i], dst_ref=piece(terms, rank, chunk),
            send_sem=back_send.at[i, slot], recv_sem=back_recv.at[rank, chunk],
            device_id=(base + i, mz), device_id_type=MESH)

    def back_own(chunk, slot):
        return pltpu.make_async_copy(
            outgo.at[slot, mine], piece(terms, rank, chunk), back_send.at[mine, slot])

    def back_arrival(worker, chunk):
        return pltpu.make_async_remote_copy(
            src_ref=outgo.at[0, 0], dst_ref=piece(terms, worker, chunk),
            send_sem=back_send.at[0, 0], recv_sem=back_recv.at[worker, chunk],
            device_id=(first_worker + worker, mz), device_id_type=MESH)

    reach = halos.shape[2]
    halo_up = pltpu.make_async_remote_copy(
        src_ref=adjoint.at[:, pl.ds(depth - reach, reach)], dst_ref=halos.at[0],
        send_sem=halo_send.at[0], recv_sem=halo_recv.at[0],
        device_id=(me, above), device_id_type=MESH)
    halo_down = pltpu.make_async_remote_copy(
        src_ref=adjoint.at[:, pl.ds(0, reach)], dst_ref=halos.at[1],
        send_sem=halo_send.at[1], recv_sem=halo_recv.at[1],
        device_id=(me, below), device_id_type=MESH)

    def each(count, body):
        def step(i, carry):
            body(i)
            return carry
        lax.fori_loop(0, count, step, 0)

    x_copy = pltpu.make_async_copy(x_op, x_mat, tile_sem.at[0])
    tiles = rows // TILE
    local_steps = max(1, chunks // 2)
    per_step = -(-tiles // local_steps)

    def arrive():
        x_copy.wait()
        halo_up.wait_recv()
        halo_down.wait_recv()

    def local_tile(t):
        strip = pl.ds(pl.multiple_of(t * TILE, TILE), TILE)
        moves = [
            pltpu.make_async_copy(halos.at[0, :, :, strip, :], ext.at[:, pl.ds(0, reach)], tile_sem.at[1]),
            pltpu.make_async_copy(adjoint.at[:, :, strip, :], ext.at[:, pl.ds(reach, depth)], tile_sem.at[2]),
            pltpu.make_async_copy(halos.at[1, :, :, strip, :], ext.at[:, pl.ds(reach + depth, reach)], tile_sem.at[3]),
            pltpu.make_async_copy(speed.at[:, strip, :], pace_tile, tile_sem.at[4]),
        ]
        for move in moves:
            move.start()
        for move in moves:
            move.wait()
        local_terms(x_mat, ext, along, pace_tile, coupling, result)
        store = pltpu.make_async_copy(result, local.at[:, :, strip, :], tile_sem.at[5])
        store.start()
        store.wait()

    @pl.when(jnp.logical_not(is_worker))
    def _():
        def send(chunk):
            @pl.when(chunk >= 2)
            def _():
                each(workers, lambda w: gather(w, chunk - 2).wait_send())
            each(workers, lambda w: gather(w, chunk).start())

            @pl.when(chunk == 0)
            def _():
                each(workers, lambda w: speed_copy(w).start())
                halo_up.start()
                halo_down.start()
                x_copy.start()
        each(chunks, send)
        arrive()
        each(tiles, local_tile)
        for last in (chunks - 2, chunks - 1):
            each(workers, lambda w: gather(w, last).wait_send())
        each(workers, lambda w: speed_copy(w).wait_send())
        each(chunks, lambda c: each(workers, lambda w: back_arrival(w, c).wait_recv()))

    @pl.when(is_worker)
    def _():
        def to_mates(chunk):
            def one(w):
                @pl.when(w != rank)
                def _():
                    gather(w, chunk).start()
            each(workers, one)
            own(chunk).start()
        each(chunks, to_mates)

        def mates(fn):
            def one(w):
                @pl.when(w != rank)
                def _():
                    fn(w)
            each(workers, one)

        def others(fn):
            def one(i):
                @pl.when(i != mine)
                def _():
                    fn(i)
            each(half_n, one)

        mates(lambda w: speed_copy(w).start())
        own_speed = pltpu.make_async_copy(
            speed.at[pl.ds(rank * planes, planes)], speeds.at[mine], op_sem.at[1])
        own_speed.start()
        op_row = pl.multiple_of(half * half_rows, half_rows)
        op_copy = pltpu.make_async_copy(
            y_ops.at[:, pl.ds(op_row, half_rows)], op_stage, op_sem.at[0])
        op_copy.start()

        def send_forward(chunk):
            own(chunk).wait()
            forward(mine, chunk).start()

            def step(k):
                i = lax.rem(k + (1 - half) * workers, half_n)

                @pl.when(i != mine)
                def _():
                    gathered(i, chunk).wait_recv()
                    forward(i, chunk).start()
            each(half_n, step)

        send_forward(0)
        halo_up.start()
        halo_down.start()
        x_copy.start()
        op_copy.wait()

        def prepare(i):
            top = pl.multiple_of(i * rows, rows)
            for op in range(2):
                high, low = split(op_stage[op, pl.ds(top, rows), :])
                lhs[i, op * rows:(op + 1) * rows, :] = high
                lhs[i, (2 + op) * rows:(3 + op) * rows, :] = low
        each(half_n, prepare)
        own_speed.wait()
        others(lambda i: speed_arrival(i).wait_recv())

        def work(chunk):
            @pl.when(chunk + 1 < chunks)
            def _():
                @pl.when(chunk >= 1)
                def _():
                    each(half_n, lambda i: forward(i, chunk - 1).wait_send())
                send_forward(chunk + 1)

            each(half_n, lambda i: forwarded(i, chunk).wait_recv())

            def convert(b):
                top = pl.multiple_of(b * rows, rows)
                for f in range(fields):
                    high, low = split(gath[chunk, b, f])
                    rhs_high[pl.ds(top, rows), f * LANES:(f + 1) * LANES] = high
                    rhs_low[pl.ds(top, rows), f * LANES:(f + 1) * LANES] = low
            each(n, convert)
            slot = lax.rem(chunk, 2)
            plane = chunk // cuts
            lane = pl.multiple_of(lax.rem(chunk, cuts) * LANES, LANES)

            @pl.when(chunk >= 2)
            def _():
                others(lambda i: back(i, chunk - 2, slot).wait_send())
                back_own(chunk - 2, slot).wait()

            def produce(k):
                i = k + half * (half_n - 1 - 2 * k)
                full = jnp.dot(lhs[i], rhs_high[...], preferred_element_type=jnp.float32)
                rest = jnp.dot(lhs[i, :2 * rows], rhs_low[...], preferred_element_type=jnp.float32)
                both = full[:2 * rows] + full[2 * rows:] + rest
                pace = speeds[i, plane, :, pl.ds(lane, LANES)]
                for f in range(fields):
                    total = coupling[0, 1, f] * both[:rows, :LANES]
                    for g in range(1, fields):
                        total = total + coupling[g, 1, f] * both[:rows, g * LANES:(g + 1) * LANES]
                    outgo[slot, i, f] = (stepping * pace) * total + (
                        stepping * viscous) * both[rows:, f * LANES:(f + 1) * LANES]

                @pl.when(i != mine)
                def _():
                    back(i, chunk, slot).start()

                @pl.when(i == mine)
                def _():
                    back_own(chunk, slot).start()
            each(half_n, produce)

            @pl.when(chunk == chunks - 1 - local_steps)
            def _():
                arrive()

            @pl.when(jnp.logical_and(chunk >= chunks - 1 - local_steps, chunk < chunks - 1))
            def _():
                first = (chunk - (chunks - 1 - local_steps)) * per_step

                def one(k):
                    @pl.when(first + k < tiles)
                    def _():
                        local_tile(first + k)
                each(per_step, one)
        each(chunks, work)

        for last in (chunks - 2, chunks - 1):
            each(half_n, lambda i: forward(i, last).wait_send())
            others(lambda i: back(i, last, last % 2).wait_send())
            back_own(last, last % 2).wait()
        each(chunks, lambda c: mates(lambda w: gather(w, c).wait_send()))
        mates(lambda w: speed_copy(w).wait_send())
        each(chunks, lambda c: mates(lambda w: back_arrival(w, c).wait_recv()))

    halo_up.wait_send()
    halo_down.wait_send()


def local_terms(x_mat, ext, along, pace_tile, coupling, result):
    fields, depth, tile, width = result.shape
    reach = len(stencil)
    x_high, x_low = split(x_mat[...])
    contract = (((1,), (1,)), ((), ()))

    def times(left, right):
        return lax.dot_general(left, right, contract, preferred_element_type=jnp.float32)

    for f in range(fields):
        high, low = split(ext[f, reach:reach + depth].reshape(depth * tile, width))
        product = times(high, x_high) + times(high, x_low) + times(low, x_high)
        along[f] = product.reshape(depth, tile, width)

    def plane(p, carry):
        across = []
        for g in range(fields):
            total = None
            for step, weight in enumerate(stencil):
                part = weight * (ext[g, p + reach + step + 1] - ext[g, p + reach - step - 1])
                total = part if total is None else total + part
            across.append(total)
        pace = stepping * pace_tile[p]
        for f in range(fields):
            total = coupling[0, 0, f] * along[0, p] + coupling[0, 2, f] * across[0]
            for g in range(1, fields):
                total = total + coupling[g, 0, f] * along[g, p] + coupling[g, 2, f] * across[g]
            result[f, p] = ext[f, p + reach] + pace * total
        return carry
    lax.fori_loop(0, depth, plane, 0)


def shards(n, nz, adjoint, speed, x_derivative, y_operators, coupling):
    fields, depth, rows, width = adjoint.shape
    half_n, workers = n // 2, n // 4
    planes = depth // workers
    chunks = planes * (width // LANES)
    reach = len(stencil)
    extent = y_operators.shape[1]
    f32, bf16 = jnp.float32, jnp.bfloat16
    dma = pltpu.SemaphoreType.DMA
    hbm = pl.BlockSpec(memory_space=pl.ANY)
    smem = pl.BlockSpec(memory_space=pltpu.SMEM)
    terms, halos, local = pl.pallas_call(
        functools.partial(y_kernel, n, nz),
        out_shape=(
            jax.ShapeDtypeStruct(adjoint.shape, f32),
            jax.ShapeDtypeStruct((2, fields, reach, rows, width), f32),
            jax.ShapeDtypeStruct(adjoint.shape, f32),
        ),
        in_specs=[hbm, hbm, hbm, hbm, smem],
        out_specs=(hbm, hbm, hbm),
        scratch_shapes=[
            pltpu.VMEM((chunks, n, fields, rows, LANES), f32),
            pltpu.VMEM((half_n, planes, rows, width), f32),
            pltpu.VMEM((2, extent // 2, extent), f32),
            pltpu.VMEM((half_n, 4 * rows, extent), bf16),
            pltpu.VMEM((extent, fields * LANES), bf16),
            pltpu.VMEM((extent, fields * LANES), bf16),
            pltpu.VMEM((2, half_n, fields, rows, LANES), f32),
            pltpu.VMEM((width, width), f32),
            pltpu.VMEM((fields, depth + 2 * reach, TILE, width), f32),
            pltpu.VMEM((fields, depth, TILE, width), f32),
            pltpu.VMEM((depth, TILE, width), f32),
            pltpu.VMEM((fields, depth, TILE, width), f32),
            dma((workers, chunks)), dma((half_n, chunks)),
            dma((half_n, chunks)), dma((half_n, chunks)),
            dma((half_n, 2)), dma((workers, chunks)),
            dma((workers,)), dma((half_n,)),
            dma((2,)), dma((2,)), dma((chunks,)), dma((2,)), dma((6,)),
        ],
        compiler_params=pltpu.CompilerParams(
            collective_id=0, has_side_effects=True, vmem_limit_bytes=56 * 2**20),
        cost_estimate=pl.CostEstimate(
            flops=12 * fields * depth * rows * width * extent,
            bytes_accessed=16 * fields * depth * rows * width, transcendentals=0),
    )(adjoint, speed, y_operators, x_derivative, jnp.transpose(coupling, (1, 0, 2)))
    return local + terms


def solution(mesh):
    placed = (P(None, "gz", "gy", None), P("gz", "gy", None), P(), P(), P())
    body = functools.partial(shards, mesh.shape["gy"], mesh.shape["gz"])
    return jax.shard_map(
        body, mesh=mesh, in_specs=placed, out_specs=P(None, "gz", "gy", None), check_vma=False
    )
```

```python
import functools

import jax
import jax.numpy as jnp
from jax import lax
from jax.experimental import pallas as pl
from jax.experimental.pallas import tpu as pltpu
from jax.sharding import PartitionSpec as P

stencil = (0.8, -0.2, 4.0 / 105.0, -1.0 / 280.0)
viscous = 0.5
stepping = 0.5
MESH = pl.DeviceIdType.MESH
LANES = 128
TILE = 16


def split(values):
    high = values.astype(jnp.bfloat16)
    low = (values - high.astype(jnp.float32)).astype(jnp.bfloat16)
    return high, low


def y_kernel(
    n, nz, adjoint, speed, y_ops, x_op, coupling, out, halos,
    gath, speeds, op_stage, lhs, rhs_high, rhs_low, outgo,
    x_mat, ext, along, pace_tile, terms, total_terms,
    gather_send, gather_recv, forward_send, forward_recv, back_send, back_recv,
    speed_send, speed_recv, halo_send, halo_recv, local_sem, op_sem, tile_sem, out_sem,
):
    fields, depth, rows, width = adjoint.shape
    half_n = n // 2
    workers = n // 4
    planes = depth // workers
    cuts = width // LANES
    chunks = planes * cuts
    me = lax.axis_index("gy")
    mz = lax.axis_index("gz")
    half = me // half_n
    mine = me - half * half_n
    base = half * half_n
    first_worker = base + (1 - half) * workers
    rank = me - first_worker
    is_worker = jnp.logical_and(rank >= 0, rank < workers)
    partner = me + (1 - 2 * half) * workers
    above, below = lax.rem(mz + 1, nz), lax.rem(mz + nz - 1, nz)
    extent = y_ops.shape[1]
    half_rows = extent // 2

    barrier = pltpu.get_barrier_semaphore()
    for side in (above, below):
        pl.semaphore_signal(barrier, inc=1, device_id=(me, side), device_id_type=MESH)

    @pl.when(is_worker)
    def _():
        def greet(i, carry):
            @pl.when(base + i != me)
            def _():
                pl.semaphore_signal(barrier, inc=1, device_id=(base + i, mz), device_id_type=MESH)
            return carry
        lax.fori_loop(0, half_n, greet, 0)
        pl.semaphore_signal(barrier, inc=1, device_id=(partner, mz), device_id_type=MESH)
        pl.semaphore_wait(barrier, half_n + 2)

    @pl.when(jnp.logical_not(is_worker))
    def _():
        def greet(i, carry):
            pl.semaphore_signal(barrier, inc=1, device_id=(first_worker + i, mz), device_id_type=MESH)
            return carry
        lax.fori_loop(0, workers, greet, 0)
        pl.semaphore_wait(barrier, workers + 2)

    def piece(ref, worker, chunk):
        plane = worker * planes + chunk // cuts
        lane = pl.multiple_of(lax.rem(chunk, cuts) * LANES, LANES)
        return ref.at[:, plane, :, pl.ds(lane, LANES)]

    def gather(worker, chunk):
        return pltpu.make_async_remote_copy(
            src_ref=piece(adjoint, worker, chunk), dst_ref=gath.at[chunk, me],
            send_sem=gather_send.at[worker, chunk], recv_sem=gather_recv.at[mine, chunk],
            device_id=(first_worker + worker, mz), device_id_type=MESH)

    def gathered(i, chunk):
        return pltpu.make_async_remote_copy(
            src_ref=gath.at[chunk, base + i], dst_ref=gath.at[chunk, base + i],
            send_sem=gather_send.at[0, chunk], recv_sem=gather_recv.at[i, chunk],
            device_id=(partner, mz), device_id_type=MESH)

    def forward(i, chunk):
        return pltpu.make_async_remote_copy(
            src_ref=gath.at[chunk, base + i], dst_ref=gath.at[chunk, base + i],
            send_sem=forward_send.at[i, chunk], recv_sem=forward_recv.at[i, chunk],
            device_id=(partner, mz), device_id_type=MESH)

    def forwarded(i, chunk):
        other = (1 - half) * half_n + i
        return pltpu.make_async_remote_copy(
            src_ref=gath.at[chunk, other], dst_ref=gath.at[chunk, other],
            send_sem=forward_send.at[i, chunk], recv_sem=forward_recv.at[i, chunk],
            device_id=(partner, mz), device_id_type=MESH)

    def forward_mine(chunk):
        return pltpu.make_async_remote_copy(
            src_ref=piece(adjoint, rank, chunk), dst_ref=gath.at[chunk, me],
            send_sem=forward_send.at[mine, chunk], recv_sem=forward_recv.at[mine, chunk],
            device_id=(partner, mz), device_id_type=MESH)

    def own(chunk):
        return pltpu.make_async_copy(piece(adjoint, rank, chunk), gath.at[chunk, me], local_sem.at[chunk])

    def speed_piece(ref, plane, chunk):
        lane = pl.multiple_of(lax.rem(chunk, cuts) * LANES, LANES)
        return ref.at[plane + chunk // cuts, :, pl.ds(lane, LANES)]

    def speed_copy(worker, chunk):
        return pltpu.make_async_remote_copy(
            src_ref=speed_piece(speed, worker * planes, chunk), dst_ref=speed_piece(speeds.at[mine], 0, chunk),
            send_sem=speed_send.at[worker, chunk], recv_sem=speed_recv.at[mine, chunk],
            device_id=(first_worker + worker, mz), device_id_type=MESH)

    def speed_arrival(i, chunk):
        return pltpu.make_async_remote_copy(
            src_ref=speed_piece(speed, 0, chunk), dst_ref=speed_piece(speeds.at[i], 0, chunk),
            send_sem=speed_send.at[0, chunk], recv_sem=speed_recv.at[i, chunk],
            device_id=(partner, mz), device_id_type=MESH)

    def back(i, chunk, slot):
        return pltpu.make_async_remote_copy(
            src_ref=outgo.at[slot, i], dst_ref=piece(terms, rank, chunk),
            send_sem=back_send.at[i, slot], recv_sem=back_recv.at[rank, chunk],
            device_id=(base + i, mz), device_id_type=MESH)

    def back_own(chunk, slot):
        return pltpu.make_async_copy(
            outgo.at[slot, mine], piece(terms, rank, chunk), back_send.at[mine, slot])

    def back_arrival(worker, chunk):
        return pltpu.make_async_remote_copy(
            src_ref=outgo.at[0, 0], dst_ref=piece(terms, worker, chunk),
            send_sem=back_send.at[0, 0], recv_sem=back_recv.at[worker, chunk],
            device_id=(first_worker + worker, mz), device_id_type=MESH)

    reach = halos.shape[2]

    def halo_up(f):
        return pltpu.make_async_remote_copy(
            src_ref=adjoint.at[f, pl.ds(depth - reach, reach)], dst_ref=halos.at[0, f],
            send_sem=halo_send.at[0, f], recv_sem=halo_recv.at[0, f],
            device_id=(me, above), device_id_type=MESH)

    def halo_down(f):
        return pltpu.make_async_remote_copy(
            src_ref=adjoint.at[f, pl.ds(0, reach)], dst_ref=halos.at[1, f],
            send_sem=halo_send.at[1, f], recv_sem=halo_recv.at[1, f],
            device_id=(me, below), device_id_type=MESH)

    def each(count, body):
        def step(i, carry):
            body(i)
            return carry
        lax.fori_loop(0, count, step, 0)

    def halo_part(step):
        def one(k):
            f = 2 * step + k

            @pl.when(f < fields)
            def _():
                halo_up(f).start()
                halo_down(f).start()
        each(2, one)

    x_copy = pltpu.make_async_copy(x_op, x_mat, tile_sem.at[0])
    tiles = rows // TILE
    local_steps = max(1, chunks // 2)
    per_step = -(-tiles // local_steps)

    def arrive():
        x_copy.wait()
        each(fields, lambda f: halo_up(f).wait_recv())
        each(fields, lambda f: halo_down(f).wait_recv())

    def local_tile(t):
        strip = pl.ds(pl.multiple_of(t * TILE, TILE), TILE)
        moves = [
            pltpu.make_async_copy(halos.at[0, :, :, strip, :], ext.at[:, pl.ds(0, reach)], tile_sem.at[1]),
            pltpu.make_async_copy(adjoint.at[:, :, strip, :], ext.at[:, pl.ds(reach, depth)], tile_sem.at[2]),
            pltpu.make_async_copy(halos.at[1, :, :, strip, :], ext.at[:, pl.ds(reach + depth, reach)], tile_sem.at[3]),
            pltpu.make_async_copy(speed.at[:, strip, :], pace_tile, tile_sem.at[4]),
        ]
        for move in moves:
            move.start()
        for move in moves:
            move.wait()
        local_terms(x_mat, ext, along, pace_tile, coupling, total_terms, t * TILE)

    def store(worker, chunk):
        return pltpu.make_async_copy(
            piece(total_terms, worker, chunk), piece(out, worker, chunk), out_sem.at[worker, chunk])

    def finish(worker, chunk):
        plane = worker * planes + chunk // cuts
        lanes = pl.ds(pl.multiple_of(lax.rem(chunk, cuts) * LANES, LANES), LANES)
        for f in range(fields):
            total_terms[f, plane, :, lanes] += terms[f, plane, :, lanes]
        store(worker, chunk).start()

    @pl.when(jnp.logical_not(is_worker))
    def _():
        def send(chunk):
            @pl.when(chunk >= 3)
            def _():
                each(workers, lambda w: gather(w, chunk - 2).wait_send())
            each(workers, lambda w: gather(w, chunk).start())
            each(workers, lambda w: speed_copy(w, chunk).start())

            @pl.when(chunk <= (fields + 1) // 2)
            def _():
                halo_part(chunk - 1)
        x_copy.start()

        def first(w):
            gather(w, 0).start()
            gather(w, 0).wait_send()
        each(workers, first)
        each(workers, lambda w: speed_copy(w, 0).start())
        each(chunks - 1, lambda c: send(c + 1))
        arrive()
        each(tiles, local_tile)
        for last in (chunks - 2, chunks - 1):
            each(workers, lambda w: gather(w, last).wait_send())
        each(chunks, lambda c: each(workers, lambda w: speed_copy(w, c).wait_send()))

        def collect(c):
            def one(w):
                back_arrival(w, c).wait_recv()
                finish(w, c)
            each(workers, one)
        each(chunks, collect)

    @pl.when(is_worker)
    def _():
        def to_mates(chunk):
            def one(w):
                @pl.when(w != rank)
                def _():
                    gather(w, chunk).start()
                    speed_copy(w, chunk).start()
            each(workers, one)
            own(chunk).start()

        def mates(fn):
            def one(w):
                @pl.when(w != rank)
                def _():
                    fn(w)
            each(workers, one)

        def others(fn):
            def one(i):
                @pl.when(i != mine)
                def _():
                    fn(i)
            each(half_n, one)

        own_speed = pltpu.make_async_copy(
            speed.at[pl.ds(rank * planes, planes)], speeds.at[mine], op_sem.at[1])
        op_row = pl.multiple_of(half * half_rows, half_rows)
        op_copy = pltpu.make_async_copy(
            y_ops.at[:, pl.ds(op_row, half_rows)], op_stage, op_sem.at[0])

        def send_forward(chunk):
            def step(k):
                i = lax.rem(k + (1 - half) * workers, half_n)

                @pl.when(i != mine)
                def _():
                    @pl.when(jnp.logical_or(chunk > 0, rank == 0))
                    def _():
                        gathered(i, chunk).wait_recv()
                    forward(i, chunk).start()
            each(half_n, step)

        to_mates(0)

        @pl.when(rank > 0)
        def _():
            others(lambda i: gathered(i, 0).wait_recv())
        forward_mine(0).start()
        own_speed.start()
        op_copy.start()
        x_copy.start()
        send_forward(0)
        to_mates(1)
        forward_mine(1).start()
        send_forward(1)
        to_mates(2)
        op_copy.wait()

        def prepare(i):
            top = pl.multiple_of(i * rows, rows)
            for op in range(2):
                high, low = split(op_stage[op, pl.ds(top, rows), :])
                lhs[i, op * rows:(op + 1) * rows, :] = high
                lhs[i, (2 + op) * rows:(3 + op) * rows, :] = low
        each(half_n, prepare)
        own_speed.wait()

        def finish_all(c):
            def one(w):
                @pl.when(w != rank)
                def _():
                    back_arrival(w, c).wait_recv()
                finish(w, c)
            each(workers, one)

        def work(chunk):
            @pl.when(chunk + 2 < chunks)
            def _():
                @pl.when(chunk >= 1)
                def _():
                    each(half_n, lambda i: forward(i, chunk - 1).wait_send())
                forward_mine(chunk + 2).start()
                send_forward(chunk + 2)

            @pl.when(chunk + 3 < chunks)
            def _():
                to_mates(chunk + 3)

            @pl.when(chunk < (fields + 1) // 2)
            def _():
                halo_part(chunk)

            slot = lax.rem(chunk, 2)

            @pl.when(chunk >= 2)
            def _():
                others(lambda i: back(i, chunk - 2, slot).wait_send())
                back_own(chunk - 2, slot).wait()

            @pl.when(chunk == chunks - 1)
            def _():
                each(chunks - 2, finish_all)

            def convert(b):
                top = pl.multiple_of(b * rows, rows)
                for f in range(fields):
                    high, low = split(gath[chunk, b, f])
                    rhs_high[pl.ds(top, rows), f * LANES:(f + 1) * LANES] = high
                    rhs_low[pl.ds(top, rows), f * LANES:(f + 1) * LANES] = low
            own(chunk).wait()
            each(half_n, lambda i: convert(base + i))

            def receive(k):
                i = lax.rem(k + half * workers, half_n)
                forwarded(i, chunk).wait_recv()
                convert((1 - half) * half_n + i)
            each(half_n, receive)
            others(lambda i: speed_arrival(i, chunk).wait_recv())
            plane = chunk // cuts
            lane = pl.multiple_of(lax.rem(chunk, cuts) * LANES, LANES)

            def produce(k):
                i = k + half * (half_n - 1 - 2 * k)
                full = jnp.dot(lhs[i], rhs_high[...], preferred_element_type=jnp.float32)
                rest = jnp.dot(lhs[i, :2 * rows], rhs_low[...], preferred_element_type=jnp.float32)
                both = full[:2 * rows] + full[2 * rows:] + rest
                pace = speeds[i, plane, :, pl.ds(lane, LANES)]
                for f in range(fields):
                    total = coupling[0, 1, f] * both[:rows, :LANES]
                    for g in range(1, fields):
                        total = total + coupling[g, 1, f] * both[:rows, g * LANES:(g + 1) * LANES]
                    outgo[slot, i, f] = (stepping * pace) * total + (
                        stepping * viscous) * both[rows:, f * LANES:(f + 1) * LANES]

                @pl.when(i != mine)
                def _():
                    back(i, chunk, slot).start()

                @pl.when(i == mine)
                def _():
                    back_own(chunk, slot).start()
            each(half_n, produce)

            @pl.when(chunk == chunks - 1 - local_steps)
            def _():
                arrive()

            @pl.when(jnp.logical_and(chunk >= chunks - 1 - local_steps, chunk < chunks - 1))
            def _():
                first = (chunk - (chunks - 1 - local_steps)) * per_step

                def one(k):
                    @pl.when(first + k < tiles)
                    def _():
                        local_tile(first + k)
                each(per_step, one)
        each(chunks, work)

        each(half_n, lambda i: forward(i, chunks - 3).wait_send())
        for last in (chunks - 2, chunks - 1):
            each(half_n, lambda i: forward(i, last).wait_send())
            others(lambda i: back(i, last, last % 2).wait_send())
            back_own(last, last % 2).wait()
        each(chunks, lambda c: mates(lambda w: gather(w, c).wait_send()))
        each(chunks, lambda c: mates(lambda w: speed_copy(w, c).wait_send()))
        finish_all(chunks - 2)
        finish_all(chunks - 1)

    each(chunks, lambda c: each(workers, lambda w: store(w, c).wait()))
    each(fields, lambda f: halo_up(f).wait_send())
    each(fields, lambda f: halo_down(f).wait_send())


def local_terms(x_mat, ext, along, pace_tile, coupling, result, top):
    fields, depth, tile, width = along.shape
    reach = len(stencil)
    x_high, x_low = split(x_mat[...])
    contract = (((1,), (1,)), ((), ()))

    def times(left, right):
        return lax.dot_general(left, right, contract, preferred_element_type=jnp.float32)

    for f in range(fields):
        high, low = split(ext[f, reach:reach + depth].reshape(depth * tile, width))
        product = times(high, x_high) + times(high, x_low) + times(low, x_high)
        along[f] = product.reshape(depth, tile, width)

    def plane(p, carry):
        across = []
        for g in range(fields):
            total = None
            for step, weight in enumerate(stencil):
                part = weight * (ext[g, p + reach + step + 1] - ext[g, p + reach - step - 1])
                total = part if total is None else total + part
            across.append(total)
        pace = stepping * pace_tile[p]
        for f in range(fields):
            total = coupling[0, 0, f] * along[0, p] + coupling[0, 2, f] * across[0]
            for g in range(1, fields):
                total = total + coupling[g, 0, f] * along[g, p] + coupling[g, 2, f] * across[g]
            result[f, p, pl.ds(pl.multiple_of(top, tile), tile), :] = ext[f, p + reach] + pace * total
        return carry
    lax.fori_loop(0, depth, plane, 0)


def shards(n, nz, adjoint, speed, x_derivative, y_operators, coupling):
    fields, depth, rows, width = adjoint.shape
    half_n, workers = n // 2, n // 4
    planes = depth // workers
    chunks = planes * (width // LANES)
    reach = len(stencil)
    extent = y_operators.shape[1]
    f32, bf16 = jnp.float32, jnp.bfloat16
    dma = pltpu.SemaphoreType.DMA
    hbm = pl.BlockSpec(memory_space=pl.ANY)
    smem = pl.BlockSpec(memory_space=pltpu.SMEM)
    out, _ = pl.pallas_call(
        functools.partial(y_kernel, n, nz),
        out_shape=(
            jax.ShapeDtypeStruct(adjoint.shape, f32),
            jax.ShapeDtypeStruct((2, fields, reach, rows, width), f32),
        ),
        in_specs=[hbm, hbm, hbm, hbm, smem],
        out_specs=(hbm, hbm),
        scratch_shapes=[
            pltpu.VMEM((chunks, n, fields, rows, LANES), f32),
            pltpu.VMEM((half_n, planes, rows, width), f32),
            pltpu.VMEM((2, extent // 2, extent), f32),
            pltpu.VMEM((half_n, 4 * rows, extent), bf16),
            pltpu.VMEM((extent, fields * LANES), bf16),
            pltpu.VMEM((extent, fields * LANES), bf16),
            pltpu.VMEM((2, half_n, fields, rows, LANES), f32),
            pltpu.VMEM((width, width), f32),
            pltpu.VMEM((fields, depth + 2 * reach, TILE, width), f32),
            pltpu.VMEM((fields, depth, TILE, width), f32),
            pltpu.VMEM((depth, TILE, width), f32),
            pltpu.VMEM(adjoint.shape, f32),
            pltpu.VMEM(adjoint.shape, f32),
            dma((workers, chunks)), dma((half_n, chunks)),
            dma((half_n, chunks)), dma((half_n, chunks)),
            dma((half_n, 2)), dma((workers, chunks)),
            dma((workers, chunks)), dma((half_n, chunks)),
            dma((2, fields)), dma((2, fields)), dma((chunks,)), dma((2,)), dma((5,)), dma((workers, chunks)),
        ],
        compiler_params=pltpu.CompilerParams(
            collective_id=0, has_side_effects=True, vmem_limit_bytes=58 * 2**20),
        cost_estimate=pl.CostEstimate(
            flops=12 * fields * depth * rows * width * extent,
            bytes_accessed=16 * fields * depth * rows * width, transcendentals=0),
    )(adjoint, speed, y_operators, x_derivative, jnp.transpose(coupling, (1, 0, 2)))
    return out


def solution(mesh):
    placed = (P(None, "gz", "gy", None), P("gz", "gy", None), P(), P(), P())
    body = functools.partial(shards, mesh.shape["gy"], mesh.shape["gz"])
    return jax.shard_map(
        body, mesh=mesh, in_specs=placed, out_specs=P(None, "gz", "gy", None), check_vma=False
    )
```
